32 devices in a mesh: groups: 1, blk: 32 (over z, y, x, core).
Axes of the slice: x: 2, y: 2, z: 4, core: 2. Of those that a mesh axis runs over, the one named last changes fastest.
Arguments:
- queries: float32 [256, 24576], P('groups', 'blk'), may hold values from -8 to 8
- cache: float32 [2048, 576], P(('groups', 'blk')), may hold values from -8 to 8
- owner: int32 [2048], P(('groups', 'blk')), may hold values from 0 to 1, as said below
- prefix_len: int32 [2], P('groups'), may hold values from 1 to 1152, as said below
- key_up: float32 [128, 512, 128], P('blk'), may hold values from -0.25 to 0.25
- value_up: float32 [128, 512, 128], P('blk'), may hold values from -0.25 to 0.25
- out_weight: float32 [16384, 7168], P('blk'), may hold values from -0.5 to 0.5
Outputs:
- mixed: float32 [256, 7168], P(('groups', 'blk'))
The draws below stay inside these ranges and needn't reach their ends.
Inputs may be any that keep to these rules, and one draw needn't show every extreme that they name: `owner`: every request owns between 768 and 1280 slots, spread over the slots in no fixed order; some request owns exactly the fewest. prefix_len[r] + 128 is at most the number of slots that request r owns.
All inputs are finite; a program needn't handle non-finite values.
Results may differ from the reference program's by a relative error of at most 0.0003.
Values sent between devices are 32-bit elements; how exact they have to be, the bound alone decides.
A program may use at most 64 MiB of HBM per device.

```python
import jax
import jax.numpy as jnp
from jax import lax

D = 7168
HEADS = 128
LATENT = 512
ROPE = 64
NOPE = 128
VDIM = 128
SPAN = 128
REQS = 2
ROWS = 256
CACHE = 2048


def plan_slots(key):
    base = jax.random.fold_in(key, 7301)
    first_key, second_key, third_key = jax.random.split(base, 3)
    chosen = jax.random.randint(jax.random.fold_in(base, 55), (), 0, REQS).astype(jnp.int32)
    req_ids = jnp.arange(REQS, dtype=jnp.int32)
    most_shift = CACHE // (4 * REQS)
    shifts = jax.random.randint(first_key, (REQS,), 0, most_shift + 1).astype(jnp.int32)
    shifts = jnp.where(req_ids == chosen, most_shift, jnp.where(req_ids == (chosen + 1) % REQS, 0, shifts)).astype(jnp.int32)
    counts = (CACHE // REQS + shifts - jnp.roll(shifts, 1)).astype(jnp.int32)
    ends = jnp.cumsum(counts)
    slot_ids = jnp.arange(CACHE, dtype=jnp.int32)
    ordered = jnp.sum((slot_ids[:, None] >= ends[None, :-1]).astype(jnp.int32), axis=1).astype(jnp.int32)
    shuffle = jax.random.permutation(second_key, CACHE)
    owners = ordered[shuffle]
    prefixes = jax.random.randint(third_key, (REQS,), 1, counts - SPAN + 1).astype(jnp.int32)
    prefixes = jnp.where(req_ids == chosen, counts - SPAN, prefixes).astype(jnp.int32)
    return (owners, prefixes)


def draw_owner(key, part):
    return plan_slots(key)[0]


def draw_prefix_len(key, part):
    return plan_slots(key)[1]


def draw_cache(key, part):
    base = jax.random.fold_in(key, 4409)
    lat_key, rope_key = jax.random.split(base)
    latent = jnp.clip(jax.random.normal(lat_key, (CACHE, LATENT), jnp.float32), -8.0, 8.0)
    rope = jnp.clip(jax.random.normal(rope_key, (CACHE, ROPE), jnp.float32), -8.0, 8.0)
    return jnp.concatenate([latent, rope], axis=1)


def draw_queries(key, part):
    width = NOPE + ROPE
    base = jax.random.fold_in(key, 6211)
    values = jnp.clip(1.5 * jax.random.normal(base, (ROWS, HEADS, width), jnp.float32), -8.0, 8.0)
    return values.reshape(ROWS, HEADS * width)


def level_of(own_key, shape, cuts, low, largest):
    def one(dim, parts):
        draws = jax.random.uniform(jax.random.fold_in(jax.random.fold_in(own_key, 6), dim), (parts,), jnp.float32, low / len(cuts), largest / len(cuts))
        return jnp.repeat(jnp.exp(draws), shape[dim] // parts).reshape((-1,) + (1,) * (len(shape) - dim - 1))

    factor_of = one(*cuts[0])
    for cut in cuts[1:]:
        factor_of = factor_of * one(*cut)
    return factor_of


def scatter_about(own_key, shape, deviation, limit, shards=(), kind=jnp.bfloat16):
    entries = jax.random.normal(own_key, shape, jnp.float32) * deviation
    if len(shards) > 0:
        entries = level_of(own_key, shape, shards, -0.22, 0.18) * entries
    return jnp.clip(entries, min=-limit, max=limit).astype(kind)


def setup_inputs(seed: int = 0, part: int = 0) -> dict:
    key_list = jax.random.split(jax.random.key(seed), 8)
    part_splits = jax.random.split(jax.random.fold_in(key_list[7], part), 8)
    queries = draw_queries(jax.random.fold_in(jax.random.fold_in(key_list[7], part), 71), part)
    cache = draw_cache(jax.random.fold_in(jax.random.fold_in(key_list[7], part), 71), part)
    owner = draw_owner(jax.random.fold_in(jax.random.fold_in(key_list[7], part), 71), part)
    prefix_len = draw_prefix_len(jax.random.fold_in(jax.random.fold_in(key_list[7], part), 71), part)
    key_up = scatter_about(key_list[4], (HEADS, LATENT, NOPE), LATENT ** -0.5, 0.25, ((0, 32),), jnp.float32)
    value_up = scatter_about(key_list[5], (HEADS, LATENT, VDIM), LATENT ** -0.5, 0.25, ((0, 32),), jnp.float32)
    out_weight = scatter_about(key_list[6], (HEADS * VDIM, D), VDIM ** -0.5, 0.5, ((0, 32),), jnp.float32)
    return {"queries": queries, "cache": cache, "owner": owner, "prefix_len": prefix_len, "key_up": key_up, "value_up": value_up, "out_weight": out_weight}


def reference(queries, cache, owner, prefix_len, key_up, value_up, out_weight):
    width = NOPE + ROPE
    hp = lax.Precision.HIGHEST
    q3 = queries.reshape(ROWS, HEADS, width)
    onehot = (owner[:, None] == jnp.arange(REQS, dtype=jnp.int32)[None, :]).astype(jnp.int32)
    position = lax.optimization_barrier(jnp.sum(onehot * (jnp.cumsum(onehot, axis=0) - 1), axis=1)).astype(jnp.int32)
    rel = (position - lax.optimization_barrier(jnp.sum(onehot * prefix_len[None, :], axis=1))).astype(jnp.int32)
    row_ids = jnp.arange(ROWS, dtype=jnp.int32)
    visible = (owner[None, :] == (row_ids // SPAN)[:, None]) & (rel[None, :] <= (row_ids % SPAN)[:, None])
    latent = cache[:, :LATENT]
    rope_keys = cache[:, LATENT:]
    scale = 1.0 / jnp.sqrt(jnp.float32(width))

    def one_head(items):
        q_head, k_up, v_up = items
        keys = jnp.dot(latent, k_up, precision=hp, preferred_element_type=jnp.float32)
        values = jnp.dot(latent, v_up, precision=hp, preferred_element_type=jnp.float32)
        score = jnp.dot(q_head[:, :NOPE], keys.T, precision=hp, preferred_element_type=jnp.float32)
        score = score + jnp.dot(q_head[:, NOPE:], rope_keys.T, precision=hp, preferred_element_type=jnp.float32)
        score = jnp.where(visible, score * scale, -jnp.inf)
        top = lax.optimization_barrier(jnp.max(score, axis=1, keepdims=True))
        expo = jnp.where(visible, jnp.exp(score - top), 0.0)
        weight = expo / lax.optimization_barrier(jnp.sum(expo, axis=1, keepdims=True))
        return jnp.dot(weight, values, precision=hp, preferred_element_type=jnp.float32)
    head_out = lax.map(one_head, (jnp.transpose(q3, (1, 0, 2)), key_up, value_up))
    flat = jnp.transpose(head_out, (1, 0, 2)).reshape(ROWS, HEADS * VDIM)
    return jnp.dot(flat, out_weight, precision=hp, preferred_element_type=jnp.float32)
```

```python
import math

import jax
import jax.numpy as jnp
from jax import lax
from jax.sharding import PartitionSpec as P

LATENT = 512
NOPE = 128
SPAN = 128
REQS = 2
CHUNKS = 4


def swap(x, bit, count):
    return lax.ppermute(x, "blk", [(i, i ^ (1 << bit)) for i in range(count)])


def bit_orders(count):
    bits = list(range(1, count.bit_length() - 1))
    low, high = bits[:2], bits[2:][::-1]
    return low + high, low[::-1] + high


def gather(block, me, count):
    rows = block.shape[0]
    parts = []
    for part, order in zip(jnp.split(block, 2, axis=0), bit_orders(count)):
        held, bits = part[None], []
        for bit in order[::-1] + [0]:
            other = swap(held, bit, count)
            mine = (me >> bit) & 1
            place = sum(1 for b in bits if b > bit)
            shape = (1 << place, -1) + part.shape
            a, b = held.reshape(shape), other.reshape(shape)
            first = jnp.where(mine == 0, a, b)
            second = jnp.where(mine == 0, b, a)
            held = jnp.stack([first, second], axis=1).reshape((-1,) + part.shape)
            bits.append(bit)
        parts.append(held)
    whole = jnp.stack(parts, axis=1)
    return whole.reshape(count * rows, block.shape[1])


def project_and_scatter(flat, weight, me, count, dot):
    rows, depth = flat.shape
    own = rows // count
    pairs = flat.reshape(count // 2, 2, own, depth)
    core = me & 1
    half = rows // 2
    away = lax.dynamic_index_in_dim(pairs, 1 - core, 1, keepdims=False).reshape(half, depth)
    home = lax.dynamic_index_in_dim(pairs, core, 1, keepdims=False).reshape(half, depth)
    width = weight.shape[1] // CHUNKS
    orders = bit_orders(count)
    outs = []
    for c in range(CHUNKS):
        part = weight[:, c * width:(c + 1) * width]
        left = dot(home, part) + swap(dot(away, part), 0, count)
        bits = list(range(1, count.bit_length() - 1))
        for bit in orders[c % 2]:
            place = sum(1 for b in bits if b > bit)
            view = left.reshape(1 << place, 2, -1, own, width)
            mine = (me >> bit) & 1
            go = lax.dynamic_index_in_dim(view, 1 - mine, 1, keepdims=False).reshape(-1, width)
            stay = lax.dynamic_index_in_dim(view, mine, 1, keepdims=False).reshape(-1, width)
            left = stay + swap(go, bit, count)
            bits.remove(bit)
        outs.append(left)
    return jnp.concatenate(outs, axis=1)


def on_device(count, queries, cache, owner, prefix_len, key_up, value_up, out_weight):
    hp = lax.Precision.HIGH
    f32 = jnp.float32
    me = lax.axis_index("blk")
    heads = key_up.shape[0]
    rows = queries.shape[0]
    width = queries.shape[1] // heads
    block = jnp.concatenate([cache, owner.astype(f32)[:, None]], axis=1)
    slab = gather(block, me, count)
    slots = slab.shape[0]
    keys = slab[:, :cache.shape[1]]
    latent = slab[:, :LATENT]
    owners = slab[:, cache.shape[1]].astype(jnp.int32)

    q3 = queries.reshape(rows, heads, width) * (1.0 / math.sqrt(width))
    q_latent = jnp.einsum("rhn,hln->hrl", q3[:, :, :NOPE], key_up, precision=hp, preferred_element_type=f32)
    q_all = jnp.concatenate([q_latent, jnp.transpose(q3[:, :, NOPE:], (1, 0, 2))], axis=2)

    lanes = math.gcd(slots, 128)
    req_ids = jnp.arange(REQS, dtype=jnp.int32)
    mine = owners[None, :] == req_ids[:, None]
    ones = mine.astype(f32).reshape(REQS, slots // lanes, lanes)
    lane = jnp.arange(lanes)
    before = (lane[:, None] < lane[None, :]).astype(f32)
    inside = jnp.einsum("rbl,lm->rbm", ones, before, precision=hp, preferred_element_type=f32)
    row = jnp.arange(slots // lanes)
    sums = jnp.sum(ones, axis=2)
    ahead = jnp.sum(jnp.where(row[None, None, :] < row[None, :, None], sums[:, None, :], 0.0), axis=2)
    position = (inside + ahead[:, :, None]).reshape(REQS, slots).astype(jnp.int32)
    rel = jnp.where(mine, position - prefix_len[:, None], jnp.int32(2**30))
    offset = jnp.arange(SPAN, dtype=jnp.int32)
    visible = (rel[:, None, :] <= offset[None, :, None]).reshape(1, rows, slots)

    score = jnp.einsum("hrl,tl->hrt", q_all, keys, precision=hp, preferred_element_type=f32)
    masked = jnp.where(visible, score, -jnp.inf)
    top = jnp.max(masked, axis=2, keepdims=True)
    expo = jnp.exp(masked - top)
    total = jnp.sum(expo, axis=2, keepdims=True)
    acc = jnp.einsum("hrt,tl->hrl", expo, latent, precision=hp, preferred_element_type=f32)
    head_out = jnp.einsum("hrl,hlv->hrv", acc / total, value_up, precision=hp, preferred_element_type=f32)
    flat = jnp.transpose(head_out, (1, 0, 2)).reshape(rows, heads * value_up.shape[2])
    dot = lambda a, b: jnp.dot(a, b, precision=hp, preferred_element_type=f32)
    return project_and_scatter(flat, out_weight, me, count, dot)


def solution(mesh):
    count = mesh.shape["blk"]
    placed = (
        P("groups", "blk"),
        P(("groups", "blk"), None),
        P(("groups", "blk")),
        P("groups"),
        P("blk", None, None),
        P("blk", None, None),
        P("blk", None),
    )
    return jax.shard_map(
        lambda *args: on_device(count, *args),
        mesh=mesh,
        in_specs=placed,
        out_specs=P(("groups", "blk"), None),
        check_vma=False,
    )
```

```python
import math

import jax
import jax.numpy as jnp
from jax import lax
from jax.sharding import PartitionSpec as P

LATENT = 512
NOPE = 128
SPAN = 128
REQS = 2
CHUNKS = 4


def swap(x, bit, count):
    return lax.ppermute(x, "blk", [(i, i ^ (1 << bit)) for i in range(count)])


def bit_orders(count):
    bits = list(range(1, count.bit_length() - 1))
    low, high = bits[:2], bits[2:][::-1]
    return low + high, low[::-1] + high


def gather(block, me, count):
    rows = block.shape[0]
    parts = []
    for part, order in zip(jnp.split(block, 2, axis=0), bit_orders(count)):
        held, bits = part[None], []
        for bit in order[::-1] + [0]:
            other = swap(held, bit, count)
            mine = (me >> bit) & 1
            place = sum(1 for b in bits if b > bit)
            shape = (1 << place, -1) + part.shape
            a, b = held.reshape(shape), other.reshape(shape)
            first = jnp.where(mine == 0, a, b)
            second = jnp.where(mine == 0, b, a)
            held = jnp.stack([first, second], axis=1).reshape((-1,) + part.shape)
            bits.append(bit)
        parts.append(held)
    whole = jnp.stack(parts, axis=1)
    return whole.reshape(count * rows, block.shape[1])


def halves(x):
    high = lax.reduce_precision(x, 8, 7)
    return high.astype(jnp.bfloat16), (x - high).astype(jnp.bfloat16)


def split_weight(weight):
    width = weight.shape[1] // CHUNKS
    return [jnp.concatenate(halves(weight[:, c * width:(c + 1) * width]), axis=0) for c in range(CHUNKS)]


def project_and_scatter(flat, weights, me, count):
    rows, depth = flat.shape
    own = rows // count
    pairs = flat.reshape(count // 2, 2, own, depth)
    core = me & 1
    half = rows // 2
    away = lax.dynamic_index_in_dim(pairs, 1 - core, 1, keepdims=False).reshape(half, depth)
    home = lax.dynamic_index_in_dim(pairs, core, 1, keepdims=False).reshape(half, depth)
    split = []
    for x in (away, home):
        high, low = halves(x)
        split += [jnp.concatenate([high, high], axis=1), low]
    split = tuple(split)

    def dot(twice, low, both):
        left = jnp.dot(twice, both, preferred_element_type=jnp.float32)
        return left + jnp.dot(low, both[:depth], preferred_element_type=jnp.float32)

    orders = bit_orders(count)
    outs = []
    for c, both in enumerate(weights):
        width = both.shape[1]
        sent = dot(*split[:2], both)
        kept = dot(*split[2:], both)
        split, kept = lax.optimization_barrier((split, kept))
        left = kept + swap(sent, 0, count)
        bits = list(range(1, count.bit_length() - 1))
        for bit in orders[c % 2]:
            place = sum(1 for b in bits if b > bit)
            view = left.reshape(1 << place, 2, -1, own, width)
            mine = (me >> bit) & 1
            go = lax.dynamic_index_in_dim(view, 1 - mine, 1, keepdims=False).reshape(-1, width)
            stay = lax.dynamic_index_in_dim(view, mine, 1, keepdims=False).reshape(-1, width)
            left = stay + swap(go, bit, count)
            bits.remove(bit)
        outs.append(left)
    return jnp.concatenate(outs, axis=1)


def on_device(count, queries, cache, owner, prefix_len, key_up, value_up, out_weight):
    hp = lax.Precision.HIGH
    f32 = jnp.float32
    me = lax.axis_index("blk")
    heads = key_up.shape[0]
    rows = queries.shape[0]
    width = queries.shape[1] // heads
    block = jnp.concatenate([cache, owner.astype(f32)[:, None]], axis=1)
    weights = split_weight(out_weight)
    slab = gather(block, me, count)
    slots = slab.shape[0]
    keys = slab[:, :cache.shape[1]]
    latent = slab[:, :LATENT]
    owners = slab[:, cache.shape[1]].astype(jnp.int32)

    q3 = queries.reshape(rows, heads, width) * (1.0 / math.sqrt(width))
    q_latent = jnp.einsum("rhn,hln->hrl", q3[:, :, :NOPE], key_up, precision=hp, preferred_element_type=f32)
    q_all = jnp.concatenate([q_latent, jnp.transpose(q3[:, :, NOPE:], (1, 0, 2))], axis=2)

    lanes = math.gcd(slots, 128)
    req_ids = jnp.arange(REQS, dtype=jnp.int32)
    mine = owners[None, :] == req_ids[:, None]
    ones = mine.astype(f32).reshape(REQS, slots // lanes, lanes)
    lane = jnp.arange(lanes)
    before = (lane[:, None] < lane[None, :]).astype(f32)
    inside = jnp.einsum("rbl,lm->rbm", ones, before, precision=hp, preferred_element_type=f32)
    row = jnp.arange(slots // lanes)
    sums = jnp.sum(ones, axis=2)
    ahead = jnp.sum(jnp.where(row[None, None, :] < row[None, :, None], sums[:, None, :], 0.0), axis=2)
    position = (inside + ahead[:, :, None]).reshape(REQS, slots).astype(jnp.int32)
    rel = jnp.where(mine, position - prefix_len[:, None], jnp.int32(2**30))
    offset = jnp.arange(SPAN, dtype=jnp.int32)
    visible = (rel[:, None, :] <= offset[None, :, None]).reshape(1, rows, slots)

    score = jnp.einsum("hrl,tl->hrt", q_all, keys, precision=hp, preferred_element_type=f32)
    masked = jnp.where(visible, score, -jnp.inf)
    top = jnp.max(masked, axis=2, keepdims=True)
    expo = jnp.exp(masked - top)
    total = jnp.sum(expo, axis=2, keepdims=True)
    acc = jnp.einsum("hrt,tl->hrl", expo, latent, precision=hp, preferred_element_type=f32)
    head_out = jnp.einsum("hrl,hlv->hrv", acc / total, value_up, precision=hp, preferred_element_type=f32)
    flat = jnp.transpose(head_out, (1, 0, 2)).reshape(rows, heads * value_up.shape[2])
    return project_and_scatter(flat, weights, me, count)


def solution(mesh):
    count = mesh.shape["blk"]
    placed = (
        P("groups", "blk"),
        P(("groups", "blk"), None),
        P(("groups", "blk")),
        P("groups"),
        P("blk", None, None),
        P("blk", None, None),
        P("blk", None),
    )
    return jax.shard_map(
        lambda *args: on_device(count, *args),
        mesh=mesh,
        in_specs=placed,
        out_specs=P(("groups", "blk"), None),
        check_vma=False,
    )
```

```python
import math

import jax
import jax.numpy as jnp
from jax import lax
from jax.sharding import PartitionSpec as P

LATENT = 512
NOPE = 128
SPAN = 128
REQS = 2
CHUNKS = 4


def swap(x, bit, count):
    return lax.ppermute(x, "blk", [(i, i ^ (1 << bit)) for i in range(count)])


def bit_orders(count):
    bits = list(range(1, count.bit_length() - 1))
    low, high = bits[:2], bits[2:][::-1]
    return low + high, low[::-1] + high, high + low


def gather(block, me, count):
    rows = block.shape[0]
    half = rows // 2
    parts, slots = [], []
    for c, part in enumerate((block[:half], block[half:])):
        held, device = part, me[None]
        for bit in bit_orders(count)[c][::-1] + [0]:
            held = jnp.concatenate([held, swap(held, bit, count)], axis=0)
            device = jnp.concatenate([device, device ^ (1 << bit)])
        parts.append(held)
        slots.append((device[:, None] * rows + c * half + jnp.arange(half, dtype=jnp.int32)).reshape(-1))
    return jnp.concatenate(parts, axis=0), jnp.concatenate(slots)


def halves(x):
    high = lax.reduce_precision(x, 8, 7)
    return high.astype(jnp.bfloat16), (x - high).astype(jnp.bfloat16)


def split_weight(weight):
    tiles = weight.shape[1] // 128
    first = tiles // 7
    step = (tiles - first) // CHUNKS
    ends = [0] + [(first + c * step) * 128 for c in range(CHUNKS)] + [weight.shape[1]]
    return [jnp.concatenate(halves(weight[:, i:j]), axis=0) for i, j in zip(ends[:-1], ends[1:])]


def project_and_scatter(flat, weights, me, count):
    rows, depth = flat.shape
    own = rows // count
    pairs = flat.reshape(count // 2, 2, own, depth)
    core = me & 1
    half = rows // 2
    away = lax.dynamic_index_in_dim(pairs, 1 - core, 1, keepdims=False).reshape(half, depth)
    home = lax.dynamic_index_in_dim(pairs, core, 1, keepdims=False).reshape(half, depth)
    split = []
    for x in (away, home):
        high, low = halves(x)
        split += [jnp.concatenate([high, high], axis=1), low]
    split = tuple(split)

    def dot(twice, low, both):
        left = jnp.dot(twice, both, preferred_element_type=jnp.float32)
        return left + jnp.dot(low, both[:depth], preferred_element_type=jnp.float32)

    paired = []
    for c, both in enumerate(weights):
        if c >= 2:
            split, paired[c - 2] = lax.optimization_barrier((split, paired[c - 2]))
        sent = dot(*split[:2], both)
        kept = dot(*split[2:], both)
        got = swap(sent, 0, count)
        split, kept = lax.optimization_barrier((split, kept))
        paired.append(kept + got)
    first, second, third = bit_orders(count)
    outs = []
    for c, left in enumerate(paired):
        width = left.shape[1]
        bits = list(range(1, count.bit_length() - 1))
        for bit in third if c == 0 else (first, second)[c % 2]:
            place = sum(1 for b in bits if b > bit)
            view = left.reshape(1 << place, 2, -1, own, width)
            mine = (me >> bit) & 1
            go = lax.dynamic_index_in_dim(view, 1 - mine, 1, keepdims=False).reshape(-1, width)
            stay = lax.dynamic_index_in_dim(view, mine, 1, keepdims=False).reshape(-1, width)
            got = swap(go, bit, count)
            if len(bits) == count.bit_length() - 2:
                got = lax.optimization_barrier((got, *paired[3:]))[0]
            left = stay + got
            bits.remove(bit)
        outs.append(left)
    return jnp.concatenate(outs, axis=1)


def on_device(count, queries, cache, owner, prefix_len, key_up, value_up, out_weight):
    hp = lax.Precision.HIGH
    f32 = jnp.float32
    me = lax.axis_index("blk")
    heads = key_up.shape[0]
    rows = queries.shape[0]
    width = queries.shape[1] // heads
    block = jnp.concatenate([cache, owner.astype(f32)[:, None]], axis=1)
    weights = split_weight(out_weight)
    slab, ids = gather(block, me, count)
    slots = slab.shape[0]
    keys = slab[:, :cache.shape[1]]
    latent = slab[:, :LATENT]
    owners = slab[:, cache.shape[1]].astype(jnp.int32)

    q3 = queries.reshape(rows, heads, width) * (1.0 / math.sqrt(width))
    q_latent = jnp.einsum("rhn,hln->hrl", q3[:, :, :NOPE], key_up, precision=hp, preferred_element_type=f32)
    q_all = jnp.concatenate([q_latent, jnp.transpose(q3[:, :, NOPE:], (1, 0, 2))], axis=2)

    req_ids = jnp.arange(REQS, dtype=jnp.int32)
    mine = owners[None, :] == req_ids[:, None]
    rank = owners * slots + ids
    below = jnp.sum((rank[:, None] < rank[None, :]).astype(jnp.int32), axis=0)
    start = jnp.sum((owners[None, :] < req_ids[:, None]).astype(jnp.int32), axis=1)
    rel = jnp.where(mine, below[None, :] - start[:, None] - prefix_len[:, None], jnp.int32(2**30))
    offset = jnp.arange(SPAN, dtype=jnp.int32)
    visible = (rel[:, None, :] <= offset[None, :, None]).reshape(1, rows, slots)

    score = jnp.einsum("hrl,tl->hrt", q_all, keys, precision=hp, preferred_element_type=f32)
    masked = jnp.where(visible, score, -jnp.inf)
    top = jnp.max(masked, axis=2, keepdims=True)
    expo = jnp.exp(masked - top)
    total = jnp.sum(expo, axis=2, keepdims=True)
    acc = jnp.einsum("hrt,tl->hrl", expo, latent, precision=hp, preferred_element_type=f32)
    head_out = jnp.einsum("hrl,hlv->hrv", acc / total, value_up, precision=hp, preferred_element_type=f32)
    flat = jnp.transpose(head_out, (1, 0, 2)).reshape(rows, heads * value_up.shape[2])
    return project_and_scatter(flat, weights, me, count)


def solution(mesh):
    count = mesh.shape["blk"]
    placed = (
        P("groups", "blk"),
        P(("groups", "blk"), None),
        P(("groups", "blk")),
        P("groups"),
        P("blk", None, None),
        P("blk", None, None),
        P("blk", None),
    )
    return jax.shard_map(
        lambda *args: on_device(count, *args),
        mesh=mesh,
        in_specs=placed,
        out_specs=P(("groups", "blk"), None),
        check_vma=False,
    )
```

```python
import math

import jax
import jax.numpy as jnp
from jax import lax
from jax.sharding import PartitionSpec as P

LATENT = 512
NOPE = 128
SPAN = 128
REQS = 2
CHUNKS = 4


def swap(x, bit, count):
    return lax.ppermute(x, "blk", [(i, i ^ (1 << bit)) for i in range(count)])


def bit_orders(count):
    bits = list(range(1, count.bit_length() - 1))
    low, high = bits[:2], bits[2:][::-1]
    return low + high, low[::-1] + high


def gather(block, me, count):
    rows = block.shape[0]
    parts = []
    for part, order in zip(jnp.split(block, 2, axis=0), bit_orders(count)):
        held, bits = part[None], []
        for bit in order[::-1] + [0]:
            other = swap(held, bit, count)
            mine = (me >> bit) & 1
            place = sum(1 for b in bits if b > bit)
            shape = (1 << place, -1) + part.shape
            a, b = held.reshape(shape), other.reshape(shape)
            first = jnp.where(mine == 0, a, b)
            second = jnp.where(mine == 0, b, a)
            held = jnp.stack([first, second], axis=1).reshape((-1,) + part.shape)
            bits.append(bit)
        parts.append(held)
    whole = jnp.stack(parts, axis=1)
    return whole.reshape(count * rows, block.shape[1])


def halves(x):
    high = lax.reduce_precision(x, 8, 7)
    return high.astype(jnp.bfloat16), (x - high).astype(jnp.bfloat16)


def split_weight(weight):
    width = weight.shape[1] // CHUNKS
    return [jnp.concatenate(halves(weight[:, c * width:(c + 1) * width]), axis=0) for c in range(CHUNKS)]


def project_and_scatter(flat, weights, me, count):
    rows, depth = flat.shape
    own = rows // count
    pairs = flat.reshape(count // 2, 2, own, depth)
    core = me & 1
    half = rows // 2
    away = lax.dynamic_index_in_dim(pairs, 1 - core, 1, keepdims=False).reshape(half, depth)
    home = lax.dynamic_index_in_dim(pairs, core, 1, keepdims=False).reshape(half, depth)
    split = []
    for x in (away, home):
        high, low = halves(x)
        split += [jnp.concatenate([high, high], axis=1), low]
    split = tuple(split)

    def dot(twice, low, both):
        left = jnp.dot(twice, both, preferred_element_type=jnp.float32)
        return left + jnp.dot(low, both[:depth], preferred_element_type=jnp.float32)

    orders = bit_orders(count)
    paired, outs = [], []
    for c, both in enumerate(weights):
        if c >= 2:
            split, paired[c - 2] = lax.optimization_barrier((split, paired[c - 2]))
        sent = dot(*split[:2], both)
        kept = dot(*split[2:], both)
        split, kept = lax.optimization_barrier((split, kept))
        paired.append(kept + swap(sent, 0, count))
    for c, left in enumerate(paired):
        width = left.shape[1]
        bits = list(range(1, count.bit_length() - 1))
        for bit in orders[c % 2]:
            place = sum(1 for b in bits if b > bit)
            view = left.reshape(1 << place, 2, -1, own, width)
            mine = (me >> bit) & 1
            go = lax.dynamic_index_in_dim(view, 1 - mine, 1, keepdims=False).reshape(-1, width)
            stay = lax.dynamic_index_in_dim(view, mine, 1, keepdims=False).reshape(-1, width)
            left = stay + swap(go, bit, count)
            bits.remove(bit)
        outs.append(left)
    return jnp.concatenate(outs, axis=1)


def on_device(count, queries, cache, owner, prefix_len, key_up, value_up, out_weight):
    hp = lax.Precision.HIGH
    f32 = jnp.float32
    me = lax.axis_index("blk")
    heads = key_up.shape[0]
    rows = queries.shape[0]
    width = queries.shape[1] // heads
    block = jnp.concatenate([cache, owner.astype(f32)[:, None]], axis=1)
    weights = split_weight(out_weight)
    slab = gather(block, me, count)
    slots = slab.shape[0]
    keys = slab[:, :cache.shape[1]]
    latent = slab[:, :LATENT]
    owners = slab[:, cache.shape[1]].astype(jnp.int32)

    q3 = queries.reshape(rows, heads, width) * (1.0 / math.sqrt(width))
    q_latent = jnp.einsum("rhn,hln->hrl", q3[:, :, :NOPE], key_up, precision=hp, preferred_element_type=f32)
    q_all = jnp.concatenate([q_latent, jnp.transpose(q3[:, :, NOPE:], (1, 0, 2))], axis=2)

    lanes = math.gcd(slots, 128)
    req_ids = jnp.arange(REQS, dtype=jnp.int32)
    mine = owners[None, :] == req_ids[:, None]
    ones = mine.astype(f32).reshape(REQS, slots // lanes, lanes)
    lane = jnp.arange(lanes)
    before = (lane[:, None] < lane[None, :]).astype(f32)
    inside = jnp.einsum("rbl,lm->rbm", ones, before, precision=hp, preferred_element_type=f32)
    row = jnp.arange(slots // lanes)
    sums = jnp.sum(ones, axis=2)
    ahead = jnp.sum(jnp.where(row[None, None, :] < row[None, :, None], sums[:, None, :], 0.0), axis=2)
    position = (inside + ahead[:, :, None]).reshape(REQS, slots).astype(jnp.int32)
    rel = jnp.where(mine, position - prefix_len[:, None], jnp.int32(2**30))
    offset = jnp.arange(SPAN, dtype=jnp.int32)
    visible = (rel[:, None, :] <= offset[None, :, None]).reshape(1, rows, slots)

    score = jnp.einsum("hrl,tl->hrt", q_all, keys, precision=hp, preferred_element_type=f32)
    masked = jnp.where(visible, score, -jnp.inf)
    top = jnp.max(masked, axis=2, keepdims=True)
    expo = jnp.exp(masked - top)
    total = jnp.sum(expo, axis=2, keepdims=True)
    acc = jnp.einsum("hrt,tl->hrl", expo, latent, precision=hp, preferred_element_type=f32)
    head_out = jnp.einsum("hrl,hlv->hrv", acc / total, value_up, precision=hp, preferred_element_type=f32)
    flat = jnp.transpose(head_out, (1, 0, 2)).reshape(rows, heads * value_up.shape[2])
    return project_and_scatter(flat, weights, me, count)


def solution(mesh):
    count = mesh.shape["blk"]
    placed = (
        P("groups", "blk"),
        P(("groups", "blk"), None),
        P(("groups", "blk")),
        P("groups"),
        P("blk", None, None),
        P("blk", None, None),
        P("blk", None),
    )
    return jax.shard_map(
        lambda *args: on_device(count, *args),
        mesh=mesh,
        in_specs=placed,
        out_specs=P(("groups", "blk"), None),
        check_vma=False,
    )
```
